32 devices in a mesh: groups: 2 (over y), feat: 4 (over z), ex: 4 (over x, core).
Axes of the slice: x: 2, y: 2, z: 4, core: 2. Of those that a mesh axis runs over, the one named last changes fastest.
Arguments:
- queries: float32 [512, 65536], P(('groups', 'ex'), 'feat'), parts along dimension 0, may hold values from -6 to 6
- eigenvalues: float32 [65536], P('feat'), may hold values from 0.05 to 5
- train_grads: bfloat16 [16384, 65536], P(('groups', 'ex'), 'feat'), parts along dimension 0, may hold values from -0.0234375 to 0.0234375
- query_index: int32 [512], P(('groups', 'ex')), parts along dimension 0, may hold values from 0 to 63, as said below
- train_index: int32 [16384], P(('groups', 'ex')), parts along dimension 0, may hold values from 0 to 2047, as said below
Outputs:
- scores: float32 [256, 16384], P('feat', ('groups', 'ex')), parts along dimension 1
The draws below stay inside these ranges and needn't reach their ends.
There are 2 independent parts, one for each index of `groups`. The reference program is written for one: setup_inputs(seed, part) draws one part's arguments, and reference() takes and returns one part's arrays. A program takes and returns all parts, laid end to end along the dimension named above; an argument that names none is the same for every part. Nothing has to cross between parts.
Inputs may be any that keep to these rules, and one draw needn't show every extreme that they name: `query_index`: within each aligned block of 64 entries every value appears exactly once. `train_index`: within each aligned block of 2048 entries every value appears exactly once.
All inputs are finite; a program needn't handle non-finite values.
Results may differ from the reference program's by a relative error of at most 0.0029.
Values may be sent and summed in bfloat16 or wider, within the bound.
A program may use at most 192 MiB of HBM per device.

```python
import math
import jax
import jax.numpy as jnp

F = 65536
NQ = 256
R_DEV = 2048
ROWS = 8192
QB = 64


def draw_query_index(key, part):
    key = jax.random.fold_in(key, 11)
    keys = jax.random.split(key, NQ // QB)
    blocks = jax.vmap(lambda sub: jax.random.permutation(sub, QB))(keys)
    return blocks.reshape(-1).astype(jnp.int32)


def draw_train_index(key, part):
    key = jax.random.fold_in(key, 23)
    keys = jax.random.split(key, ROWS // R_DEV)
    blocks = jax.vmap(lambda sub: jax.random.permutation(sub, R_DEV))(keys)
    return blocks.reshape(-1).astype(jnp.int32)


def spiked(drawn, own_key, source, target, parts, factor):
    def block_of(position):
        return (jnp.arange(drawn.shape[position]) // (drawn.shape[position] // parts)).reshape((-1,) + (1,) * (drawn.ndim - 1 - position))

    first = jax.random.permutation(own_key, parts)[block_of(target)]
    far = (block_of(target) + parts // 2) % parts
    return jnp.where((block_of(source) == first) | (block_of(source) == far), factor * drawn, drawn)


def shard_levels(key, extent, shards, least, top_value):
    loudness = 1.0
    for position, parts in shards:
        steps = jax.random.uniform(jax.random.fold_in(jax.random.fold_in(key, 6), position), (parts,), jnp.float32, least / len(shards), top_value / len(shards))
        loudness = loudness * jnp.repeat(jnp.exp(steps), extent[position] // parts).reshape((-1,) + (1,) * (len(extent) - 1 - position))
    return loudness


def centred(rng, shape, width, bound, cuts=(), kind=jnp.bfloat16):
    values = width * jax.random.normal(rng, shape, jnp.float32)
    if cuts:
        values = values * shard_levels(rng, shape, cuts, -0.22, 0.18)
    return jnp.clip(values, -bound, bound).astype(kind)


def noise_with(rng, dims, spread, reach, cuts, heavy, held_as=jnp.bfloat16):
    entries = spread * jax.random.normal(rng, dims, jnp.float32)
    if cuts:
        entries = entries * shard_levels(rng, dims, cuts, -0.22, 0.18)
    return jnp.clip(spiked(entries, jax.random.fold_in(rng, 3), *heavy), -reach, reach).astype(held_as)


def setup_inputs(seed: int = 0, part: int = 0) -> dict:
    streams_of = jax.random.split(jax.random.key(seed), 6)
    part_keys = jax.random.split(jax.random.fold_in(streams_of[5], part), 6)
    queries = noise_with(part_keys[0], (NQ, F), 1.0, 6.0, ((0, 4), (1, 4)), (1, 0, 4, 2.0), jnp.float32)
    eigenvalues = jnp.clip(jnp.exp(math.log(5.0) - 4.6051702 * jax.random.uniform(streams_of[1], (F,), jnp.float32) ** shard_levels(streams_of[1], (F,), ((0, 4),), -0.2, 0.2)), 0.05, 5.0)
    train_grads = centred(part_keys[2], (ROWS, F), F ** -0.5, 0.0234375, ((0, 4), (1, 4)))
    query_index = draw_query_index(jax.random.fold_in(jax.random.fold_in(streams_of[5], part), 71), part)
    train_index = draw_train_index(jax.random.fold_in(jax.random.fold_in(streams_of[5], part), 71), part)
    return {"queries": queries, "eigenvalues": eigenvalues, "train_grads": train_grads, "query_index": query_index, "train_index": train_index}


damping = 0.05


def reference(queries, eigenvalues, train_grads, query_index, train_index):
    query_rows = (jnp.arange(NQ, dtype=jnp.int32) // QB) * QB + query_index.astype(jnp.int32)
    selected = jnp.take(queries, query_rows, axis=0)
    scaled = (selected / (eigenvalues + damping)[None, :]).astype(jnp.bfloat16)
    raw = jnp.dot(scaled, train_grads.T, preferred_element_type=jnp.float32)
    train_rows = (jnp.arange(ROWS, dtype=jnp.int32) // R_DEV) * R_DEV + train_index.astype(jnp.int32)
    return jnp.take(raw, train_rows, axis=1)
```

```python
import jax
import jax.numpy as jnp
from jax import lax
from jax.experimental import pallas as pl
from jax.experimental.pallas import tpu as pltpu
from jax.sharding import PartitionSpec as P

damping = 0.05


def from_behind(block, axis, distance):
    devices = range(lax.axis_size(axis))
    route = [((i - distance) % len(devices), i) for i in devices]
    return lax.ppermute(block, axis, route)


def products(left, train_grads):
    return lax.dot_general(
        left, train_grads, (((1,), (1,)), ((), ())), preferred_element_type=jnp.float32
    )


def ring_local(queries, eigenvalues, train_grads, query_index, train_index):
    block_size = queries.shape[0]
    local_rows = train_grads.shape[0]
    cycle_size = lax.axis_size("ex")
    total_queries = block_size * cycle_size
    selected = jnp.take(queries, query_index, axis=0)
    scaled = (selected / (eigenvalues + damping)[None, :]).astype(jnp.bfloat16)
    partial_value = jnp.zeros((total_queries, local_rows), jnp.float32)
    resident = scaled
    position = lax.axis_index("ex")
    for turn in range(cycle_size):
        block_id = (position - turn) % cycle_size
        partial_value = lax.dynamic_update_slice_in_dim(
            partial_value, products(resident, train_grads), block_id * block_size, 0
        )
        if turn + 1 < cycle_size:
            resident = from_behind(resident, "ex", 1)
    summed = lax.psum_scatter(partial_value, "feat", scatter_dimension=0, tiled=True)
    return jnp.take(summed, train_index, axis=1)


WIDTH = 1024
WINDOW = 6
KEPT = 4
SLOTS = 3
HALVES = 2
MESH = pl.DeviceIdType.MESH


def kernel(
    queries, eigenvalues, query_index, train_index, train, out,
    stack, acc, order, kept, ring, outgoing, incoming,
    kept_sem, ring_sem, far_send, far_recv, fwd_send, fwd_recv,
    sib_send, sib_recv, sum_send, sum_recv,
):
    me = lax.axis_index("ex")
    z = lax.axis_index("feat")
    sib = me + 1 - 2 * lax.rem(me, 2)
    far = lax.rem(me + 2, 4)
    far_sib = lax.rem(sib + 2, 4)
    rows = queries.shape[0]
    half = rows // HALVES
    chunks = queries.shape[1] // WIDTH
    total = HALVES * chunks
    local_rows = train.shape[0]
    feats = incoming.shape[0]

    barrier = pltpu.get_barrier_semaphore()
    pl.semaphore_signal(barrier, inc=1, device_id={"ex": sib}, device_id_type=MESH)
    pl.semaphore_signal(barrier, inc=1, device_id={"ex": far}, device_id_type=MESH)
    for d in range(1, feats):
        pl.semaphore_signal(barrier, inc=1, device_id={"feat": lax.rem(z + d, feats)}, device_id_type=MESH)

    def columns(k):
        return pl.ds(pl.multiple_of(k * WIDTH, WIDTH), WIDTH)

    def place(owner, j):
        return stack.at[j // chunks, pl.ds(pl.multiple_of(owner * half, half), half), columns(j % chunks)]

    def to_far(j):
        return pltpu.make_async_remote_copy(
            place(me, j), place(me, j), far_send.at[j], far_recv.at[j], device_id={"ex": far}, device_id_type=MESH)

    def from_far(j):
        return pltpu.make_async_remote_copy(
            place(far, j), place(far, j), far_send.at[j], far_recv.at[j], device_id={"ex": far}, device_id_type=MESH)

    def to_sib(j):
        return pltpu.make_async_remote_copy(
            place(me, j), place(me, j), sib_send.at[j], sib_recv.at[j], device_id={"ex": sib}, device_id_type=MESH)

    def from_sib(j):
        return pltpu.make_async_remote_copy(
            place(sib, j), place(sib, j), sib_send.at[j], sib_recv.at[j], device_id={"ex": sib}, device_id_type=MESH)

    def forward(j):
        return pltpu.make_async_remote_copy(
            place(far, j), place(far, j), fwd_send.at[j], fwd_recv.at[j], device_id={"ex": sib}, device_id_type=MESH)

    def forwarded(j):
        return pltpu.make_async_remote_copy(
            place(far_sib, j), place(far_sib, j), fwd_send.at[j], fwd_recv.at[j], device_id={"ex": sib}, device_id_type=MESH)

    streamed = chunks - KEPT

    def keep(k):
        return pltpu.make_async_copy(train.at[:, columns(k)], kept.at[k], kept_sem.at[k])

    def stream(s):
        return pltpu.make_async_copy(
            train.at[:, columns(KEPT + lax.rem(s, streamed))], ring.at[lax.rem(s, SLOTS)], ring_sem.at[lax.rem(s, SLOTS)])

    for k in range(KEPT):
        keep(k).start()
    for s in range(SLOTS):
        stream(jnp.int32(s)).start()

    lanes = lax.broadcasted_iota(jnp.int32, (rows, rows), 1)
    pick = (query_index[...] == lanes).astype(jnp.float32).astype(jnp.bfloat16)

    def scale(k):
        inverse = 1.0 / (eigenvalues[:, columns(k)] + damping)
        scaled = (queries[:, columns(k)] * inverse).astype(jnp.bfloat16)
        selected = jnp.dot(pick, scaled, preferred_element_type=jnp.float32).astype(jnp.bfloat16)
        mine = pl.ds(pl.multiple_of(me * half, half), half)
        for h in range(HALVES):
            stack[h, mine, columns(k)] = selected[h * half:(h + 1) * half]

    scale(0)
    pl.semaphore_wait(barrier, feats + 1)

    def first(k, carry):
        to_far(k).start()
        to_sib(k).start()
        to_sib(chunks + k).start()
        scale(k + 1)
        return carry

    def later(k, carry):
        scale(k)
        to_sib(k).start()
        to_sib(chunks + k).start()
        return carry

    lax.fori_loop(0, WINDOW - 1, first, 0)
    to_far(WINDOW - 1).start()
    to_sib(WINDOW - 1).start()
    to_sib(chunks + WINDOW - 1).start()
    lax.fori_loop(WINDOW, chunks, later, 0)

    from_far(0).wait_recv()
    forward(0).start()
    to_far(WINDOW).start()
    acc[...] = jnp.zeros_like(acc)

    tile = 256
    def build(i, carry):
        at = pl.ds(pl.multiple_of(i * tile, tile), tile)
        positions = lax.broadcasted_iota(jnp.int32, (tile, local_rows), 0) + i * tile
        order[at, :] = (train_index[...] == positions).astype(jnp.float32).astype(jnp.bfloat16)
        return carry

    lax.fori_loop(0, local_rows // tile, build, 0)

    def ready(j):
        @pl.when(j + 1 < total)
        def _():
            from_far(j + 1).wait_recv()
            forward(j + 1).start()

        @pl.when(j + 1 + WINDOW < total)
        def _():
            to_far(j + 1 + WINDOW).start()

        from_sib(j).wait_recv()
        forwarded(j).wait_recv()

    def multiply(h, k, block):
        acc[h] += lax.dot_general(
            stack[h, :, columns(k)], block[...], (((1,), (1,)), ((), ())),
            preferred_element_type=jnp.float32)

    def sums(h, d):
        to = lax.rem(z + d, feats)
        n = h * (feats - 1) + d - 1
        return pltpu.make_async_remote_copy(
            outgoing.at[h, pl.ds(pl.multiple_of(to * half, half), half), :], incoming.at[z, h],
            sum_send.at[n], sum_recv.at[n], device_id={"feat": to}, device_id_type=MESH)

    def arriving(h, d):
        n = h * (feats - 1) + d - 1
        return pltpu.make_async_remote_copy(
            incoming.at[lax.rem(z - d + feats, feats), h], incoming.at[lax.rem(z - d + feats, feats), h],
            sum_send.at[n], sum_recv.at[n], device_id={"feat": lax.rem(z + d, feats)}, device_id_type=MESH)

    for h in range(HALVES):
        def from_kept(k, carry, h=h):
            ready(h * chunks + k)
            if h == 0:
                keep(k).wait()
            multiply(h, k, kept.at[k])
            return carry

        def from_ring(k, carry, h=h):
            s = h * streamed + k - KEPT
            ready(h * chunks + k)
            stream(s).wait()
            multiply(h, k, ring.at[lax.rem(s, SLOTS)])

            @pl.when(s + SLOTS < HALVES * streamed)
            def _():
                stream(s + SLOTS).start()
            return carry

        lax.fori_loop(0, KEPT, from_kept, 0)
        lax.fori_loop(KEPT, chunks, from_ring, 0)

        def arrange(i, carry, h=h):
            at = pl.ds(pl.multiple_of(i * tile, tile), tile)
            outgoing[h, :, at] = jnp.dot(
                acc[h].astype(jnp.bfloat16), order[:, at],
                preferred_element_type=jnp.float32).astype(jnp.bfloat16)
            return carry

        lax.fori_loop(0, local_rows // tile, arrange, 0)
        for d in range(1, feats):
            sums(h, d).start()

    for h in range(HALVES):
        summed = outgoing[h, pl.ds(pl.multiple_of(z * half, half), half), :].astype(jnp.float32)
        for d in range(1, feats):
            arriving(h, d).wait_recv()
            summed += incoming[lax.rem(z - d + feats, feats), h].astype(jnp.float32)
        out[h * half:(h + 1) * half, :] = summed

    def drain(j, carry):
        to_far(j).wait_send()
        to_sib(j).wait_send()
        forward(j).wait_send()
        return carry

    lax.fori_loop(0, total, drain, 0)
    for h in range(HALVES):
        for d in range(1, feats):
            sums(h, d).wait_send()


def local(queries, eigenvalues, train_grads, query_index, train_index):
    rows, features = queries.shape
    feats = lax.axis_size("feat")
    local_rows = train_grads.shape[0]
    if lax.axis_size("ex") != 4 or feats != 4 or features < 8 * WIDTH:
        return ring_local(queries, eigenvalues, train_grads, query_index, train_index)
    half = rows // HALVES
    total = HALVES * (features // WIDTH)
    vmem = pl.BlockSpec(memory_space=pltpu.VMEM)
    links = HALVES * (feats - 1)
    return pl.pallas_call(
        kernel,
        out_shape=jax.ShapeDtypeStruct((rows, local_rows), jnp.float32),
        in_specs=[vmem, vmem, vmem, vmem, pl.BlockSpec(memory_space=pl.ANY)],
        out_specs=vmem,
        scratch_shapes=[
            pltpu.VMEM((HALVES, 4 * half, features), jnp.bfloat16),
            pltpu.VMEM((HALVES, 4 * half, local_rows), jnp.float32),
            pltpu.VMEM((local_rows, local_rows), jnp.bfloat16),
            pltpu.VMEM((KEPT, local_rows, WIDTH), jnp.bfloat16),
            pltpu.VMEM((SLOTS, local_rows, WIDTH), jnp.bfloat16),
            pltpu.VMEM((HALVES, 4 * half, local_rows), jnp.bfloat16),
            pltpu.VMEM((feats, HALVES, half, local_rows), jnp.bfloat16),
            pltpu.SemaphoreType.DMA((KEPT,)),
            pltpu.SemaphoreType.DMA((SLOTS,)),
        ] + [pltpu.SemaphoreType.DMA((total,))] * 6 + [pltpu.SemaphoreType.DMA((links,))] * 2,
        compiler_params=pltpu.CompilerParams(
            collective_id=0, has_side_effects=True, vmem_limit_bytes=60 * 1024 * 1024),
        name="scores",
    )(queries, eigenvalues.reshape(1, -1), query_index.reshape(-1, 1), train_index.reshape(1, -1), train_grads)


def solution(mesh):
    return jax.shard_map(
        local,
        mesh=mesh,
        in_specs=(
            P(("groups", "ex"), "feat"),
            P("feat"),
            P(("groups", "ex"), "feat"),
            P(("groups", "ex")),
            P(("groups", "ex")),
        ),
        out_specs=P("feat", ("groups", "ex")),
        check_vma=False,
    )
```

```python
import jax
import jax.numpy as jnp
from jax import lax
from jax.experimental import pallas as pl
from jax.experimental.pallas import tpu as pltpu
from jax.sharding import PartitionSpec as P

damping = 0.05


def from_behind(block, axis, distance):
    devices = range(lax.axis_size(axis))
    route = [((i - distance) % len(devices), i) for i in devices]
    return lax.ppermute(block, axis, route)


def products(left, train_grads):
    return lax.dot_general(
        left, train_grads, (((1,), (1,)), ((), ())), preferred_element_type=jnp.float32
    )


def ring_local(queries, eigenvalues, train_grads, query_index, train_index):
    block_size = queries.shape[0]
    local_rows = train_grads.shape[0]
    cycle_size = lax.axis_size("ex")
    total_queries = block_size * cycle_size
    selected = jnp.take(queries, query_index, axis=0)
    scaled = (selected / (eigenvalues + damping)[None, :]).astype(jnp.bfloat16)
    partial_value = jnp.zeros((total_queries, local_rows), jnp.float32)
    resident = scaled
    position = lax.axis_index("ex")
    for turn in range(cycle_size):
        block_id = (position - turn) % cycle_size
        partial_value = lax.dynamic_update_slice_in_dim(
            partial_value, products(resident, train_grads), block_id * block_size, 0
        )
        if turn + 1 < cycle_size:
            resident = from_behind(resident, "ex", 1)
    summed = lax.psum_scatter(partial_value, "feat", scatter_dimension=0, tiled=True)
    return jnp.take(summed, train_index, axis=1)


WIDTH = 1024
WINDOW = 12
KEPT = 4
SLOTS = 3
HALVES = 2
PIECES = 4
MESH = pl.DeviceIdType.MESH


def kernel(
    eigenvalues, query_index, train_index, queries_hbm, train, out,
    queries, stack, acc, order, kept, ring, outgoing, incoming,
    kept_sem, ring_sem, far_send, far_recv, fwd_send, fwd_recv,
    sib_send, sib_recv, query_sem, sum_send, sum_recv,
):
    me = lax.axis_index("ex")
    z = lax.axis_index("feat")
    sib = me + 1 - 2 * lax.rem(me, 2)
    far = lax.rem(me + 2, 4)
    far_sib = lax.rem(sib + 2, 4)
    rows = queries.shape[0]
    half = rows // HALVES
    chunks = queries.shape[1] // WIDTH
    total = HALVES * chunks
    local_rows = train.shape[0]
    feats = incoming.shape[0]

    barrier = pltpu.get_barrier_semaphore()
    pl.semaphore_signal(barrier, inc=1, device_id={"ex": sib}, device_id_type=MESH)
    pl.semaphore_signal(barrier, inc=1, device_id={"ex": far}, device_id_type=MESH)
    for d in range(1, feats):
        pl.semaphore_signal(barrier, inc=1, device_id={"feat": lax.rem(z + d, feats)}, device_id_type=MESH)

    def columns(k):
        return pl.ds(pl.multiple_of(k * WIDTH, WIDTH), WIDTH)

    def place(owner, j):
        return stack.at[j // chunks, pl.ds(pl.multiple_of(owner * half, half), half), columns(j % chunks)]

    def to_far(j):
        return pltpu.make_async_remote_copy(
            place(me, j), place(me, j), far_send.at[j], far_recv.at[j], device_id={"ex": far}, device_id_type=MESH)

    def from_far(j):
        return pltpu.make_async_remote_copy(
            place(far, j), place(far, j), far_send.at[j], far_recv.at[j], device_id={"ex": far}, device_id_type=MESH)

    def to_sib(j):
        return pltpu.make_async_remote_copy(
            place(me, j), place(me, j), sib_send.at[j], sib_recv.at[j], device_id={"ex": sib}, device_id_type=MESH)

    def from_sib(j):
        return pltpu.make_async_remote_copy(
            place(sib, j), place(sib, j), sib_send.at[j], sib_recv.at[j], device_id={"ex": sib}, device_id_type=MESH)

    def forward(j):
        return pltpu.make_async_remote_copy(
            place(far, j), place(far, j), fwd_send.at[j], fwd_recv.at[j], device_id={"ex": sib}, device_id_type=MESH)

    def forwarded(j):
        return pltpu.make_async_remote_copy(
            place(far_sib, j), place(far_sib, j), fwd_send.at[j], fwd_recv.at[j], device_id={"ex": sib}, device_id_type=MESH)

    streamed = chunks - KEPT

    def keep(k):
        return pltpu.make_async_copy(train.at[:, columns(k)], kept.at[k], kept_sem.at[k])

    def stream(s):
        return pltpu.make_async_copy(
            train.at[:, columns(KEPT + lax.rem(s, streamed))], ring.at[lax.rem(s, SLOTS)], ring_sem.at[lax.rem(s, SLOTS)])

    def load(k):
        return pltpu.make_async_copy(queries_hbm.at[:, columns(k)], queries.at[:, columns(k)], query_sem.at[k])

    for k in range(chunks):
        load(k).start()
    for k in range(chunks):
        load(k).wait()
    for k in range(KEPT):
        keep(k).start()
    for s in range(SLOTS):
        stream(jnp.int32(s)).start()

    sources = lax.broadcasted_iota(jnp.int32, (rows, rows), 0)
    pick = (query_index[...] == sources).astype(jnp.float32).astype(jnp.bfloat16)

    def scale(k):
        inverse = 1.0 / (eigenvalues[:, columns(k)] + damping)
        scaled = (queries[:, columns(k)] * inverse).astype(jnp.bfloat16)
        selected = lax.dot_general(
            pick, scaled, (((0,), (0,)), ((), ())), preferred_element_type=jnp.float32).astype(jnp.bfloat16)
        mine = pl.ds(pl.multiple_of(me * half, half), half)
        for h in range(HALVES):
            stack[h, mine, columns(k)] = selected[h * half:(h + 1) * half]

    scale(0)
    pl.semaphore_wait(barrier, feats + 1)

    def first(k, carry):
        to_far(k).start()
        to_sib(k).start()
        to_sib(chunks + k).start()
        scale(k + 1)
        return carry

    def later(k, carry):
        scale(k)
        to_sib(k).start()
        to_sib(chunks + k).start()
        return carry

    lax.fori_loop(0, WINDOW - 1, first, 0)
    to_far(WINDOW - 1).start()
    to_sib(WINDOW - 1).start()
    to_sib(chunks + WINDOW - 1).start()
    lax.fori_loop(WINDOW, chunks, later, 0)

    from_far(0).wait_recv()
    forward(0).start()
    to_far(WINDOW).start()
    acc[...] = jnp.zeros_like(acc)

    tile = 256
    def build(i, carry):
        at = pl.ds(pl.multiple_of(i * tile, tile), tile)
        positions = lax.broadcasted_iota(jnp.int32, (tile, local_rows), 0) + i * tile
        order[at, :] = (train_index[...] == positions).astype(jnp.float32).astype(jnp.bfloat16)
        return carry

    lax.fori_loop(0, local_rows // tile, build, 0)

    def ready(j):
        @pl.when(j + 1 < total)
        def _():
            from_far(j + 1).wait_recv()
            forward(j + 1).start()

        @pl.when(j + 1 + WINDOW < total)
        def _():
            to_far(j + 1 + WINDOW).start()

        from_sib(j).wait_recv()
        forwarded(j).wait_recv()

    def multiply(h, k, block):
        acc[h] += lax.dot_general(
            block[...], stack[h, :, columns(k)], (((1,), (1,)), ((), ())),
            preferred_element_type=jnp.float32)

    part = local_rows // PIECES

    def piece(i):
        return pl.ds(pl.multiple_of(i * part, part), part)

    def number(h, d, i):
        return (h * (feats - 1) + d - 1) * PIECES + i

    def partner(d):
        return {1: z + 1 - 2 * lax.rem(z, 2), 2: lax.rem(z + 2, 4), 3: 3 - z}[d]

    def sums(h, d, i):
        to = partner(d)
        n = number(h, d, i)
        return pltpu.make_async_remote_copy(
            outgoing.at[h, pl.ds(pl.multiple_of(to * half, half), half), piece(i)], incoming.at[z, h, :, piece(i)],
            sum_send.at[n], sum_recv.at[n], device_id={"feat": to}, device_id_type=MESH)

    def arriving(h, d, i):
        n = number(h, d, i)
        source = partner(d)
        return pltpu.make_async_remote_copy(
            incoming.at[source, h, :, piece(i)], incoming.at[source, h, :, piece(i)],
            sum_send.at[n], sum_recv.at[n], device_id={"feat": source}, device_id_type=MESH)

    for h in range(HALVES):
        def from_kept(k, carry, h=h):
            ready(h * chunks + k)
            if h == 0:
                keep(k).wait()
            multiply(h, k, kept.at[k])
            return carry

        def from_ring(k, carry, h=h):
            s = h * streamed + k - KEPT
            ready(h * chunks + k)
            stream(s).wait()
            multiply(h, k, ring.at[lax.rem(s, SLOTS)])

            @pl.when(s + SLOTS < HALVES * streamed)
            def _():
                stream(s + SLOTS).start()
            return carry

        lax.fori_loop(0, KEPT, from_kept, 0)
        lax.fori_loop(KEPT, chunks, from_ring, 0)

        turned = acc[h].T.astype(jnp.bfloat16)

        def arrange(i, carry, h=h):
            outgoing[h, :, piece(i)] = jnp.dot(
                turned, order[:, piece(i)], preferred_element_type=jnp.float32).astype(jnp.bfloat16)
            for d in (2, 3, 1):
                sums(h, d, i).start()
            return carry

        lax.fori_loop(0, PIECES, arrange, 0)

    for h in range(HALVES):
        def gather(i, carry, h=h):
            summed = outgoing[h, pl.ds(pl.multiple_of(z * half, half), half), piece(i)].astype(jnp.float32)
            for d in (1, 2, 3):
                arriving(h, d, i).wait_recv()
                summed += incoming[partner(d), h, :, piece(i)].astype(jnp.float32)
            out[h * half:(h + 1) * half, piece(i)] = summed
            return carry

        lax.fori_loop(0, PIECES, gather, 0)

    def drain(j, carry):
        to_far(j).wait_send()
        to_sib(j).wait_send()
        forward(j).wait_send()
        return carry

    lax.fori_loop(0, total, drain, 0)
    for h in range(HALVES):
        for d in range(1, feats):
            for i in range(PIECES):
                sums(h, d, i).wait_send()


def local(queries, eigenvalues, train_grads, query_index, train_index):
    rows, features = queries.shape
    feats = lax.axis_size("feat")
    local_rows = train_grads.shape[0]
    if lax.axis_size("ex") != 4 or feats != 4 or features < 8 * WIDTH:
        return ring_local(queries, eigenvalues, train_grads, query_index, train_index)
    half = rows // HALVES
    total = HALVES * (features // WIDTH)
    vmem = pl.BlockSpec(memory_space=pltpu.VMEM)
    links = HALVES * (feats - 1) * PIECES
    return pl.pallas_call(
        kernel,
        out_shape=jax.ShapeDtypeStruct((rows, local_rows), jnp.float32),
        in_specs=[vmem, vmem, vmem] + [pl.BlockSpec(memory_space=pl.ANY)] * 2,
        out_specs=vmem,
        scratch_shapes=[
            pltpu.VMEM((rows, features), jnp.float32),
            pltpu.VMEM((HALVES, 4 * half, features), jnp.bfloat16),
            pltpu.VMEM((HALVES, local_rows, 4 * half), jnp.float32),
            pltpu.VMEM((local_rows, local_rows), jnp.bfloat16),
            pltpu.VMEM((KEPT, local_rows, WIDTH), jnp.bfloat16),
            pltpu.VMEM((SLOTS, local_rows, WIDTH), jnp.bfloat16),
            pltpu.VMEM((HALVES, 4 * half, local_rows), jnp.bfloat16),
            pltpu.VMEM((feats, HALVES, half, local_rows), jnp.bfloat16),
            pltpu.SemaphoreType.DMA((KEPT,)),
            pltpu.SemaphoreType.DMA((SLOTS,)),
        ] + [pltpu.SemaphoreType.DMA((total,))] * 6 + [pltpu.SemaphoreType.DMA((features // WIDTH,))] + [pltpu.SemaphoreType.DMA((links,))] * 2,
        compiler_params=pltpu.CompilerParams(
            collective_id=0, has_side_effects=True, vmem_limit_bytes=60 * 1024 * 1024),
        name="scores",
    )(eigenvalues.reshape(1, -1), query_index.reshape(1, -1), train_index.reshape(1, -1), queries, train_grads)


def solution(mesh):
    return jax.shard_map(
        local,
        mesh=mesh,
        in_specs=(
            P(("groups", "ex"), "feat"),
            P("feat"),
            P(("groups", "ex"), "feat"),
            P(("groups", "ex")),
            P(("groups", "ex")),
        ),
        out_specs=P("feat", ("groups", "ex")),
        check_vma=False,
    )
```

```python
import jax
import jax.numpy as jnp
from jax import lax
from jax.experimental import pallas as pl
from jax.experimental.pallas import tpu as pltpu
from jax.sharding import PartitionSpec as P

damping = 0.05


def from_behind(block, axis, distance):
    devices = range(lax.axis_size(axis))
    route = [((i - distance) % len(devices), i) for i in devices]
    return lax.ppermute(block, axis, route)


def products(left, train_grads):
    return lax.dot_general(
        left, train_grads, (((1,), (1,)), ((), ())), preferred_element_type=jnp.float32
    )


def ring_local(queries, eigenvalues, train_grads, query_index, train_index):
    block_size = queries.shape[0]
    local_rows = train_grads.shape[0]
    cycle_size = lax.axis_size("ex")
    total_queries = block_size * cycle_size
    selected = jnp.take(queries, query_index, axis=0)
    scaled = (selected / (eigenvalues + damping)[None, :]).astype(jnp.bfloat16)
    partial_value = jnp.zeros((total_queries, local_rows), jnp.float32)
    resident = scaled
    position = lax.axis_index("ex")
    for turn in range(cycle_size):
        block_id = (position - turn) % cycle_size
        partial_value = lax.dynamic_update_slice_in_dim(
            partial_value, products(resident, train_grads), block_id * block_size, 0
        )
        if turn + 1 < cycle_size:
            resident = from_behind(resident, "ex", 1)
    summed = lax.psum_scatter(partial_value, "feat", scatter_dimension=0, tiled=True)
    return jnp.take(summed, train_index, axis=1)


WIDTH = 1024
WINDOW = 12
KEPT = 4
SLOTS = 3
HALVES = 2
PIECES = 4
MESH = pl.DeviceIdType.MESH


def kernel(
    eigenvalues, query_index, train_index, queries_hbm, train, out,
    queries, stack, acc, order, kept, ring, outgoing, incoming,
    kept_sem, ring_sem, far_send, far_recv, fwd_send, fwd_recv,
    sib_send, sib_recv, query_sem, sum_send, sum_recv,
):
    me = lax.axis_index("ex")
    z = lax.axis_index("feat")
    sib = me + 1 - 2 * lax.rem(me, 2)
    far = lax.rem(me + 2, 4)
    far_sib = lax.rem(sib + 2, 4)
    rows = queries.shape[0]
    half = rows // HALVES
    chunks = queries.shape[1] // WIDTH
    total = HALVES * chunks
    local_rows = train.shape[0]
    feats = incoming.shape[0]

    barrier = pltpu.get_barrier_semaphore()
    pl.semaphore_signal(barrier, inc=1, device_id={"ex": sib}, device_id_type=MESH)
    pl.semaphore_signal(barrier, inc=1, device_id={"ex": far}, device_id_type=MESH)
    for d in range(1, feats):
        pl.semaphore_signal(barrier, inc=1, device_id={"feat": lax.rem(z + d, feats)}, device_id_type=MESH)

    def columns(k):
        return pl.ds(pl.multiple_of(k * WIDTH, WIDTH), WIDTH)

    def place(owner, j):
        return stack.at[j // chunks, pl.ds(pl.multiple_of(owner * half, half), half), columns(j % chunks)]

    def to_far(j):
        return pltpu.make_async_remote_copy(
            place(me, j), place(me, j), far_send.at[j], far_recv.at[j], device_id={"ex": far}, device_id_type=MESH)

    def from_far(j):
        return pltpu.make_async_remote_copy(
            place(far, j), place(far, j), far_send.at[j], far_recv.at[j], device_id={"ex": far}, device_id_type=MESH)

    def to_sib(j):
        return pltpu.make_async_remote_copy(
            place(me, j), place(me, j), sib_send.at[j], sib_recv.at[j], device_id={"ex": sib}, device_id_type=MESH)

    def from_sib(j):
        return pltpu.make_async_remote_copy(
            place(sib, j), place(sib, j), sib_send.at[j], sib_recv.at[j], device_id={"ex": sib}, device_id_type=MESH)

    def forward(j):
        return pltpu.make_async_remote_copy(
            place(far, j), place(far, j), fwd_send.at[j], fwd_recv.at[j], device_id={"ex": sib}, device_id_type=MESH)

    def forwarded(j):
        return pltpu.make_async_remote_copy(
            place(far_sib, j), place(far_sib, j), fwd_send.at[j], fwd_recv.at[j], device_id={"ex": sib}, device_id_type=MESH)

    streamed = chunks - KEPT

    def keep(k):
        return pltpu.make_async_copy(train.at[:, columns(k)], kept.at[k], kept_sem.at[k])

    def stream(s):
        return pltpu.make_async_copy(
            train.at[:, columns(KEPT + lax.rem(s, streamed))], ring.at[lax.rem(s, SLOTS)], ring_sem.at[lax.rem(s, SLOTS)])

    def load(k):
        return pltpu.make_async_copy(queries_hbm.at[:, columns(k)], queries.at[:, columns(k)], query_sem.at[k])

    for k in range(chunks):
        load(k).start()
    for k in range(chunks):
        load(k).wait()

    sources = lax.broadcasted_iota(jnp.int32, (rows, rows), 0)
    pick = (query_index[...] == sources).astype(jnp.float32).astype(jnp.bfloat16)

    def scale(k):
        inverse = 1.0 / (eigenvalues[:, columns(k)] + damping)
        scaled = (queries[:, columns(k)] * inverse).astype(jnp.bfloat16)
        selected = lax.dot_general(
            pick, scaled, (((0,), (0,)), ((), ())), preferred_element_type=jnp.float32).astype(jnp.bfloat16)
        mine = pl.ds(pl.multiple_of(me * half, half), half)
        for h in range(HALVES):
            stack[h, mine, columns(k)] = selected[h * half:(h + 1) * half]

    scale(0)
    for k in range(KEPT):
        keep(k).start()
    for s in range(SLOTS):
        stream(jnp.int32(s)).start()
    pl.semaphore_wait(barrier, feats + 1)

    def first(k, carry):
        to_far(k).start()
        to_sib(k).start()
        to_sib(chunks + k).start()
        scale(k + 1)
        return carry

    def later(k, carry):
        scale(k)
        to_sib(k).start()
        to_sib(chunks + k).start()
        return carry

    lax.fori_loop(0, WINDOW - 1, first, 0)
    to_far(WINDOW - 1).start()
    to_sib(WINDOW - 1).start()
    to_sib(chunks + WINDOW - 1).start()
    lax.fori_loop(WINDOW, chunks, later, 0)

    from_far(0).wait_recv()
    forward(0).start()
    to_far(WINDOW).start()
    acc[...] = jnp.zeros_like(acc)

    tile = 256
    def build(i, carry):
        at = pl.ds(pl.multiple_of(i * tile, tile), tile)
        positions = lax.broadcasted_iota(jnp.int32, (tile, local_rows), 0) + i * tile
        order[at, :] = (train_index[...] == positions).astype(jnp.float32).astype(jnp.bfloat16)
        return carry

    lax.fori_loop(0, local_rows // tile, build, 0)

    def ready(j):
        @pl.when(j + 1 < total)
        def _():
            from_far(j + 1).wait_recv()
            forward(j + 1).start()

        @pl.when(j + 1 + WINDOW < total)
        def _():
            to_far(j + 1 + WINDOW).start()

        from_sib(j).wait_recv()
        forwarded(j).wait_recv()

    def multiply(h, k, block):
        acc[h] += lax.dot_general(
            block[...], stack[h, :, columns(k)], (((1,), (1,)), ((), ())),
            preferred_element_type=jnp.float32)

    part = local_rows // PIECES

    def piece(i):
        return pl.ds(pl.multiple_of(i * part, part), part)

    def number(h, d, i):
        return (h * (feats - 1) + d - 1) * PIECES + i

    def partner(d):
        return {1: z + 1 - 2 * lax.rem(z, 2), 2: lax.rem(z + 2, 4), 3: 3 - z}[d]

    def sums(h, d, i):
        to = partner(d)
        n = number(h, d, i)
        return pltpu.make_async_remote_copy(
            outgoing.at[h, pl.ds(pl.multiple_of(to * half, half), half), piece(i)], incoming.at[z, h, :, piece(i)],
            sum_send.at[n], sum_recv.at[n], device_id={"feat": to}, device_id_type=MESH)

    def arriving(h, d, i):
        n = number(h, d, i)
        source = partner(d)
        return pltpu.make_async_remote_copy(
            incoming.at[source, h, :, piece(i)], incoming.at[source, h, :, piece(i)],
            sum_send.at[n], sum_recv.at[n], device_id={"feat": source}, device_id_type=MESH)

    for h in range(HALVES):
        def from_kept(k, carry, h=h):
            ready(h * chunks + k)
            if h == 0:
                keep(k).wait()
            multiply(h, k, kept.at[k])
            return carry

        def from_ring(k, carry, h=h):
            s = h * streamed + k - KEPT
            ready(h * chunks + k)
            stream(s).wait()
            multiply(h, k, ring.at[lax.rem(s, SLOTS)])

            @pl.when(s + SLOTS < HALVES * streamed)
            def _():
                stream(s + SLOTS).start()
            return carry

        lax.fori_loop(0, KEPT, from_kept, 0)
        lax.fori_loop(KEPT, chunks, from_ring, 0)

        turned = acc[h].T.astype(jnp.bfloat16)

        def arrange(i, carry, h=h):
            outgoing[h, :, piece(i)] = jnp.dot(
                turned, order[:, piece(i)], preferred_element_type=jnp.float32).astype(jnp.bfloat16)
            for d in (2, 3, 1):
                sums(h, d, i).start()
            return carry

        lax.fori_loop(0, PIECES, arrange, 0)

    for h in range(HALVES):
        def gather(i, carry, h=h):
            summed = outgoing[h, pl.ds(pl.multiple_of(z * half, half), half), piece(i)].astype(jnp.float32)
            for d in (1, 2, 3):
                arriving(h, d, i).wait_recv()
                summed += incoming[partner(d), h, :, piece(i)].astype(jnp.float32)
            out[h * half:(h + 1) * half, piece(i)] = summed
            return carry

        lax.fori_loop(0, PIECES, gather, 0)

    def drain(j, carry):
        to_far(j).wait_send()
        to_sib(j).wait_send()
        forward(j).wait_send()
        return carry

    lax.fori_loop(0, total, drain, 0)
    for h in range(HALVES):
        for d in range(1, feats):
            for i in range(PIECES):
                sums(h, d, i).wait_send()


def local(queries, eigenvalues, train_grads, query_index, train_index):
    rows, features = queries.shape
    feats = lax.axis_size("feat")
    local_rows = train_grads.shape[0]
    if lax.axis_size("ex") != 4 or feats != 4 or features < 8 * WIDTH:
        return ring_local(queries, eigenvalues, train_grads, query_index, train_index)
    half = rows // HALVES
    total = HALVES * (features // WIDTH)
    vmem = pl.BlockSpec(memory_space=pltpu.VMEM)
    links = HALVES * (feats - 1) * PIECES
    return pl.pallas_call(
        kernel,
        out_shape=jax.ShapeDtypeStruct((rows, local_rows), jnp.float32),
        in_specs=[vmem, vmem, vmem] + [pl.BlockSpec(memory_space=pl.ANY)] * 2,
        out_specs=vmem,
        scratch_shapes=[
            pltpu.VMEM((rows, features), jnp.float32),
            pltpu.VMEM((HALVES, 4 * half, features), jnp.bfloat16),
            pltpu.VMEM((HALVES, local_rows, 4 * half), jnp.float32),
            pltpu.VMEM((local_rows, local_rows), jnp.bfloat16),
            pltpu.VMEM((KEPT, local_rows, WIDTH), jnp.bfloat16),
            pltpu.VMEM((SLOTS, local_rows, WIDTH), jnp.bfloat16),
            pltpu.VMEM((HALVES, 4 * half, local_rows), jnp.bfloat16),
            pltpu.VMEM((feats, HALVES, half, local_rows), jnp.bfloat16),
            pltpu.SemaphoreType.DMA((KEPT,)),
            pltpu.SemaphoreType.DMA((SLOTS,)),
        ] + [pltpu.SemaphoreType.DMA((total,))] * 6 + [pltpu.SemaphoreType.DMA((features // WIDTH,))] + [pltpu.SemaphoreType.DMA((links,))] * 2,
        compiler_params=pltpu.CompilerParams(
            collective_id=0, has_side_effects=True, vmem_limit_bytes=60 * 1024 * 1024),
        name="scores",
    )(eigenvalues.reshape(1, -1), query_index.reshape(1, -1), train_index.reshape(1, -1), queries, train_grads)


def solution(mesh):
    return jax.shard_map(
        local,
        mesh=mesh,
        in_specs=(
            P(("groups", "ex"), "feat"),
            P("feat"),
            P(("groups", "ex"), "feat"),
            P(("groups", "ex")),
            P(("groups", "ex")),
        ),
        out_specs=P("feat", ("groups", "ex")),
        check_vma=False,
    )
```
